32 devices in a mesh: groups: 2 (over x), shard: 8 (over z, y), sub: 2 (over core).
Axes of the slice: x: 2, y: 2, z: 4, core: 2. Of those that a mesh axis runs over, the one named last changes fastest.
Arguments:
- queries: bfloat16 [256, 32, 128], P(('groups', 'shard', 'sub')), parts along dimension 0, may hold values from -0.19921875 to 0.19921875
- documents: bfloat16 [4096, 128, 128], P(('shard', 'sub')), may hold values from -0.59765625 to 0.59765625
- doc_lengths: int32 [4096], P(('shard', 'sub')), may hold values from 1 to 128
- candidates: int32 [256, 128], P('groups', ('shard', 'sub')), parts along dimension 0, may hold values from -1 to 255, as said below
Outputs:
- scores: float32 [256, 128], P(('groups', 'shard', 'sub')), parts along dimension 0
The draws below stay inside these ranges and needn't reach their ends.
There are 2 independent parts, one for each index of `groups`. The reference program is written for one: setup_inputs(seed, part) draws one part's arguments, and reference() takes and returns one part's arrays. A program takes and returns all parts, laid end to end along the dimension named above; an argument that names none is the same for every part. Nothing has to cross between parts.
Inputs may be any that keep to these rules, and one draw needn't show every extreme that they name: `candidates`: -1 marks an empty slot; column c names a document block of device c // 8.
All inputs are finite; a program needn't handle non-finite values.
Results may differ from the reference program's by a relative error of at most 0.0003.
Values may be sent and summed in bfloat16 or wider, within the bound.
No kernel may reach another device: no remote copies, remote signals or barrier semaphores. Data moves between devices by JAX's collectives and lax.ppermute only.
A program may use at most 64 MiB of HBM per device.

```python
import jax
import jax.numpy as jnp
from jax import lax

DIM = 128
QT = 32
DT = 128
DOC_DEV = 256
SLOTS = 8
DEVS = 16
QUERIES = 128
DOCS = 4096
CANDS = 128


def draw_candidates(key, part):
    key = jax.random.fold_in(key, 7)
    key_slot, key_live, key_rate = jax.random.split(key, 3)
    slot_ids = jax.random.randint(key_slot, (QUERIES, CANDS), 0, DOC_DEV)
    device_rate = jax.random.randint(key_rate, (DEVS,), 1, 5)
    column_rate = jnp.repeat(device_rate, SLOTS)
    chance = jax.random.randint(key_live, (QUERIES, CANDS), 0, 5)
    return jnp.where(chance < column_rate[None, :], slot_ids, -1).astype(jnp.int32)


def with_ends(result, stream_key, smallest, largest):
    longest = result.shape.index(max(result.shape))
    spots = []
    for shift in (0, 1):
        where = [jax.random.randint(jax.random.fold_in(stream_key, axis), (), 0, length) for axis, length in enumerate(result.shape)]
        where[longest] = (where[longest] + shift) % result.shape[longest]
        spots.append(tuple(where))
    return result.at[spots[0]].set(smallest).at[spots[1]].set(largest)


def level_of(rng, dims, shards, least, high):
    loudness, own = 1.0, jax.random.fold_in(rng, 6)
    for position, parts in shards:
        draws = jnp.exp(jax.random.uniform(jax.random.fold_in(own, position), (parts,), jnp.float32, least / len(shards), high / len(shards)))
        loudness = loudness * jnp.repeat(draws, dims[position] // parts).reshape([-1 if axis == position else 1 for axis in range(len(dims))])
    return loudness


def noise(own_key, extent, deviation, bound, pieces=(), kind=jnp.bfloat16):
    drawn = jax.random.normal(own_key, extent, jnp.float32) * deviation
    if len(pieces) > 0:
        drawn = level_of(own_key, extent, pieces, -0.22, 0.18) * drawn
    return jnp.clip(drawn, min=-bound, max=bound).astype(kind)


def setup_inputs(seed: int = 0, part: int = 0) -> dict:
    seeds = jax.random.split(jax.random.key(seed), 5)
    own_keys = jax.random.split(jax.random.fold_in(seeds[4], part), 5)
    queries = noise(own_keys[0], (QUERIES, QT, DIM), 0.03125, 0.19921875, ((0, 16),))
    documents = noise(seeds[1], (DOCS, DT, DIM), 0.0884, 0.59765625, ((0, 16),))
    doc_lengths = with_ends(jax.random.randint(seeds[2], (DOCS,), 1, DT + 1), jax.random.fold_in(seeds[2], 1), 1, DT).astype(jnp.int32)
    candidates = draw_candidates(jax.random.fold_in(jax.random.fold_in(seeds[4], part), 71), part)
    return dict(queries=queries, documents=documents, doc_lengths=doc_lengths, candidates=candidates)


def reference(queries, documents, doc_lengths, candidates):
    column = jnp.arange(candidates.shape[1], dtype=jnp.int32)
    holder = (column // SLOTS).astype(jnp.int32)
    token_pos = jnp.arange(DT, dtype=jnp.int32)

    def score_query(pair):
        one_query, slot_ids = pair
        filled = slot_ids >= 0
        doc_rows = (holder * DOC_DEV + jnp.maximum(slot_ids, 0)).astype(jnp.int32)
        picked = documents[doc_rows].astype(jnp.float32)
        similar = jnp.einsum("td,ckd->ctk", one_query.astype(jnp.float32), picked)
        usable = token_pos[None, :] < doc_lengths[doc_rows][:, None]
        top_match = jnp.max(jnp.where(usable[:, None, :], similar, -jnp.inf), axis=2)
        return jnp.where(filled, jnp.sum(top_match, axis=1), jnp.zeros((), top_match.dtype))

    return lax.map(score_query, (queries, candidates), batch_size=8)
```

```python
import functools

import jax
import jax.numpy as jnp
from jax import lax
from jax.experimental import pallas as pl
from jax.experimental.pallas import tpu as pltpu
from jax.sharding import PartitionSpec as P

AXES = ("shard", "sub")
VMEM = pl.BlockSpec(memory_space=pltpu.VMEM)
SMEM = pl.BlockSpec(memory_space=pltpu.SMEM)


def prepare_kernel(lengths, documents, out):
    count, tokens, dim = documents.shape
    step = pl.program_id(0)
    row = lax.broadcasted_iota(jnp.int32, (tokens, dim), 0)

    @pl.when(step < pl.num_programs(0) - 1)
    def _():
        def body(i, carry):
            block = documents[i]
            out[i] = jnp.where(row < lengths[step * count + i], block, block[0:1, :])
            return carry

        lax.fori_loop(0, count, body, 0, unroll=4)

    @pl.when(step == pl.num_programs(0) - 1)
    def _():
        out[...] = jnp.zeros(out.shape, out.dtype)


def prepare(lengths, documents):
    count, tokens, dim = documents.shape
    part = 32
    steps = count // part
    size = documents.size * 2
    return pl.pallas_call(
        prepare_kernel,
        grid=(steps + 1,),
        out_shape=jax.ShapeDtypeStruct((count + part, tokens, dim), documents.dtype),
        in_specs=[SMEM, pl.BlockSpec((part, tokens, dim), lambda i: (jnp.minimum(i, steps - 1), 0, 0))],
        out_specs=pl.BlockSpec((part, tokens, dim), lambda i: (i, 0, 0)),
        compiler_params=pltpu.CompilerParams(vmem_limit_bytes=48 << 20),
        cost_estimate=pl.CostEstimate(flops=documents.size * 10, bytes_accessed=2 * size, transcendentals=0),
        name="prepare",
    )(lengths, documents)


def score_kernel(shifts, n_blocks, candidates, *refs):
    blocks, documents, outs, held = refs[:n_blocks], refs[n_blocks], refs[n_blocks + 1 : -1], refs[-1]
    me = lax.axis_index("shard") * lax.axis_size("sub") + lax.axis_index("sub")
    slots = candidates.shape[0]
    empty = documents.shape[0] - 1
    n_queries, terms, dim = blocks[0].shape
    half = slots // 2
    width = outs[0].shape[-1]
    tokens = documents.shape[1]
    for b, block in enumerate(blocks):
        held[pl.ds(b * n_queries, n_queries)] = block[...]
    lane = lax.broadcasted_iota(jnp.int32, (slots, width), 1)
    pair = lax.broadcasted_iota(jnp.int32, (slots, width), 0) % half
    at_first = lane == me * slots + pair
    at_second = lane == me * slots + half + pair
    first = lax.broadcasted_iota(jnp.int32, (slots, 2 * terms), 1) < terms
    nothing = jnp.zeros((terms, dim), documents.dtype)

    def tops(place, column):
        query = held[place]
        both = jnp.concatenate(
            [jnp.concatenate([query, nothing], 1), jnp.concatenate([nothing, query], 1)], 0
        )
        rows = []
        for s in range(slots):
            named = candidates[s, column]
            rows.append(jnp.where(named >= 0, named, empty))
        found = []
        for p in range(half):
            sides = jnp.concatenate([documents[rows[p]], documents[rows[p + half]]], 1)
            similar = lax.dot_general(
                sides, both, (((1,), (1,)), ((), ())), preferred_element_type=jnp.float32
            )
            found.append(jnp.max(similar, axis=0, keepdims=True))
        return found

    def block_scores(b, out, o):
        owner = me ^ shifts[b]
        for i in range(0, n_queries, 2):
            top = jnp.concatenate(
                tops(b * n_queries + i, owner * n_queries + i)
                + tops(b * n_queries + i + 1, owner * n_queries + i + 1),
                0,
            )
            one = jnp.sum(jnp.where(first, top, 0.0), axis=1, keepdims=True)
            two = jnp.sum(jnp.where(first, 0.0, top), axis=1, keepdims=True)
            spread = jnp.where(at_first, one, jnp.where(at_second, two, 0.0))
            out[o, i : i + 1, :] = jnp.sum(spread[:half], axis=0, keepdims=True)
            out[o, i + 1 : i + 2, :] = jnp.sum(spread[half:], axis=0, keepdims=True)

    for b in range(n_blocks):
        block_scores(b, outs[b // 2], b % 2)


def score(shifts, candidates, blocks, documents, width):
    n_blocks = len(blocks)
    n_queries, terms, dim = blocks[0].shape
    tokens = documents.shape[1]
    pairs = n_blocks * n_queries * candidates.shape[0]
    flops = 2 * pairs * terms * dim * tokens * 8
    return pl.pallas_call(
        functools.partial(score_kernel, shifts, n_blocks),
        out_shape=[jax.ShapeDtypeStruct((2, n_queries, width), jnp.float32)] * (n_blocks // 2),
        in_specs=[SMEM] + [VMEM] * (n_blocks + 1),
        out_specs=[VMEM] * (n_blocks // 2),
        scratch_shapes=[pltpu.VMEM((n_blocks * n_queries, terms, dim), blocks[0].dtype)],
        compiler_params=pltpu.CompilerParams(vmem_limit_bytes=16 << 20),
        cost_estimate=pl.CostEstimate(flops=flops, bytes_accessed=0, transcendentals=0),
        name="score",
    )(candidates, *blocks, documents)


def shards(queries, documents, doc_lengths, candidates):
    shard, sub = lax.axis_size("shard"), lax.axis_size("sub")
    devices = shard * sub

    def swap(value, k):
        return lax.ppermute(value, AXES, [(i, i ^ k) for i in range(devices)])

    width = devices * candidates.shape[1]
    columns = candidates.T
    steps = [z * 4 for z in range(shard // 2)]
    along = {z: (queries if z == 0 else swap(queries, z)) for z in reversed(steps)}
    ready = prepare(doc_lengths, documents)
    across = {z: swap(along[z], 2) for z in reversed(steps)}
    near_sum, far_sum = [], []
    for z in reversed(steps):
        blocks = [along[z], swap(along[z], 1), across[z], swap(across[z], 1)]
        near, far = score((z, z ^ 1, z ^ 2, z ^ 3), columns, blocks, ready, width)
        near_sum.append(near if z == 0 else swap(near, z))
        far_sum.append(far if z == 0 else swap(far, z))
    mine = sum(near_sum[1:], near_sum[0]) + swap(sum(far_sum[1:], far_sum[0]), 2)
    return mine[0] + swap(mine[1], 1)


def solution(mesh):
    in_specs = (
        P(("groups", "shard", "sub"), None, None),
        P(("shard", "sub"), None, None),
        P(("shard", "sub")),
        P("groups", ("shard", "sub")),
    )
    out_specs = P(("groups", "shard", "sub"), None)
    return jax.shard_map(shards, mesh=mesh, in_specs=in_specs, out_specs=out_specs, check_vma=False)
```

```python
import functools

import jax
import jax.numpy as jnp
from jax import lax
from jax.experimental import pallas as pl
from jax.experimental.pallas import tpu as pltpu
from jax.sharding import PartitionSpec as P

AXES = ("shard", "sub")
VMEM = pl.BlockSpec(memory_space=pltpu.VMEM)
SMEM = pl.BlockSpec(memory_space=pltpu.SMEM)


def score_kernel(shifts, n_blocks, candidates, lengths, *refs):
    blocks, documents, out = refs[:n_blocks], refs[n_blocks], refs[n_blocks + 1]
    me = lax.axis_index("shard") * lax.axis_size("sub") + lax.axis_index("sub")
    slots = candidates.shape[0]
    n_queries, terms, dim = blocks[0].shape
    tokens = documents.shape[1]
    width = out.shape[-1]
    group = dim // terms
    row = lax.broadcasted_iota(jnp.int32, (tokens, group * terms), 0)
    which = lax.broadcasted_iota(jnp.int32, (1, group * terms), 1) // terms
    member = lax.broadcasted_iota(jnp.int32, (group * terms, dim), 0) // terms
    lane = lax.broadcasted_iota(jnp.int32, (slots, width), 1)
    slot = lax.broadcasted_iota(jnp.int32, (slots, width), 0)
    own = lane == me * slots + slot

    def group_scores(b, first):
        column = (me ^ shifts[b]) * n_queries + first
        terms_of = blocks[b][first : first + group].reshape(group * terms, dim)
        spread = jnp.concatenate(
            [jnp.where(member == g, terms_of, jnp.zeros_like(terms_of)) for g in range(group)], 1
        )
        tops = []
        for s in range(slots):
            sides = []
            limit = jnp.zeros((1, group * terms), jnp.int32)
            for g in range(group):
                named = candidates[s, column + g]
                place = jnp.maximum(named, 0)
                sides.append(documents[place])
                limit = jnp.where(which == g, jnp.where(named >= 0, lengths[place], 0), limit)
            similar = lax.dot_general(
                jnp.concatenate(sides, 1),
                spread,
                (((1,), (1,)), ((), ())),
                preferred_element_type=jnp.float32,
            )
            tops.append(jnp.max(jnp.where(row < limit, similar, -jnp.inf), axis=0, keepdims=True))
        top = jnp.concatenate(tops, 0)
        top = jnp.where(top == -jnp.inf, 0.0, top)
        for g in range(group):
            total = jnp.sum(jnp.where(which == g, top, 0.0), axis=1, keepdims=True)
            line = jnp.sum(jnp.where(own, total, 0.0), axis=0, keepdims=True)
            out[b, first + g : first + g + 1, :] = line

    for b in range(n_blocks):
        for first in range(0, n_queries, group):
            group_scores(b, first)


def score(shifts, candidates, lengths, blocks, documents, width):
    n_blocks = len(blocks)
    n_queries, terms, dim = blocks[0].shape
    tokens = documents.shape[1]
    pairs = n_blocks * n_queries * candidates.shape[0]
    flops = 2 * pairs * terms * dim * tokens * 8
    return pl.pallas_call(
        functools.partial(score_kernel, shifts, n_blocks),
        out_shape=jax.ShapeDtypeStruct((n_blocks, n_queries, width), jnp.float32),
        in_specs=[SMEM, SMEM] + [VMEM] * (n_blocks + 1),
        out_specs=VMEM,
        compiler_params=pltpu.CompilerParams(vmem_limit_bytes=16 << 20),
        cost_estimate=pl.CostEstimate(flops=flops, bytes_accessed=0, transcendentals=0),
        name="score",
    )(candidates, lengths, *blocks, documents)


def shards(queries, documents, doc_lengths, candidates):
    shard, sub = lax.axis_size("shard"), lax.axis_size("sub")
    devices = shard * sub

    def swap(value, k):
        return lax.ppermute(value, AXES, [(i, i ^ k) for i in range(devices)])

    width = devices * candidates.shape[1]
    columns = candidates.T
    steps = [z * 4 for z in range(shard // 2)]
    along = {z: (queries if z == 0 else swap(queries, z)) for z in reversed(steps)}
    across = {z: swap(along[z], 2) for z in reversed(steps)}
    sums = []
    for z in reversed(steps):
        blocks = [along[z], swap(along[z], 1), across[z], swap(across[z], 1)]
        tiles = score((z, z ^ 1, z ^ 2, z ^ 3), columns, doc_lengths, blocks, documents, width)
        sums.append(tiles if z == 0 else swap(tiles, z))
    total = sum(sums[1:], sums[0])
    mine = total[:2] + swap(total[2:], 2)
    return mine[0] + swap(mine[1], 1)


def solution(mesh):
    in_specs = (
        P(("groups", "shard", "sub"), None, None),
        P(("shard", "sub"), None, None),
        P(("shard", "sub")),
        P("groups", ("shard", "sub")),
    )
    out_specs = P(("groups", "shard", "sub"), None)
    return jax.shard_map(shards, mesh=mesh, in_specs=in_specs, out_specs=out_specs, check_vma=False)
```

```python
import functools

import jax
import jax.numpy as jnp
from jax import lax
from jax.experimental import pallas as pl
from jax.experimental.pallas import tpu as pltpu
from jax.sharding import PartitionSpec as P

AXES = ("shard", "sub")
VMEM = pl.BlockSpec(memory_space=pltpu.VMEM)
SMEM = pl.BlockSpec(memory_space=pltpu.SMEM)


def lanes_kernel(own):
    me = lax.axis_index("shard") * lax.axis_size("sub") + lax.axis_index("sub")
    lane = lax.broadcasted_iota(jnp.int32, own.shape, 1)
    slot = lax.broadcasted_iota(jnp.int32, own.shape, 0)
    own[...] = jnp.where(lane == me * own.shape[0] + slot, 1.0, 0.0)


def lanes_of(slots, width):
    return pl.pallas_call(
        lanes_kernel,
        out_shape=jax.ShapeDtypeStruct((slots, width), jnp.float32),
        out_specs=VMEM,
        compiler_params=pltpu.CompilerParams(vmem_limit_bytes=1 << 20),
        cost_estimate=pl.CostEstimate(flops=1 << 35, bytes_accessed=0, transcendentals=0),
        name="lanes",
    )()


def score_kernel(shifts, n_blocks, candidates, lengths, own, *refs):
    blocks, documents, out = refs[:n_blocks], refs[n_blocks], refs[n_blocks + 1]
    me = lax.axis_index("shard") * lax.axis_size("sub") + lax.axis_index("sub")
    slots = candidates.shape[0]
    n_queries, terms, dim = blocks[0].shape
    tokens = documents.shape[1]
    group = dim // terms
    row = lax.broadcasted_iota(jnp.int32, (tokens, group * terms), 0)
    which = lax.broadcasted_iota(jnp.int32, (1, group * terms), 1) // terms
    member = lax.broadcasted_iota(jnp.int32, (group * terms, dim), 0) // terms
    mark = own[...]

    def group_scores(b, first):
        column = (me ^ shifts[b]) * n_queries + first
        terms_of = blocks[b][first : first + group].reshape(group * terms, dim)
        spread = jnp.concatenate(
            [jnp.where(member == g, terms_of, jnp.zeros_like(terms_of)) for g in range(group)], 1
        )
        tops = []
        for s in range(slots):
            sides = []
            limit = jnp.zeros((1, group * terms), jnp.int32)
            for g in range(group):
                named = candidates[s, column + g]
                place = jnp.maximum(named, 0)
                sides.append(documents[place])
                limit = jnp.where(which == g, jnp.where(named >= 0, lengths[place], 0), limit)
            similar = lax.dot_general(
                jnp.concatenate(sides, 1),
                spread,
                (((1,), (1,)), ((), ())),
                preferred_element_type=jnp.float32,
            )
            tops.append(jnp.max(jnp.where(row < limit, similar, -jnp.inf), axis=0, keepdims=True))
        top = jnp.concatenate(tops, 0)
        top = jnp.where(top == -jnp.inf, 0.0, top)
        for g in range(group):
            total = jnp.sum(jnp.where(which == g, top, 0.0), axis=1, keepdims=True)
            line = jnp.sum(mark * total, axis=0, keepdims=True)
            out[b, first + g : first + g + 1, :] = line

    for b in range(n_blocks):
        for first in range(0, n_queries, group):
            group_scores(b, first)


def score(shifts, candidates, lengths, own, blocks, documents):
    n_blocks = len(blocks)
    n_queries, terms, dim = blocks[0].shape
    tokens = documents.shape[1]
    pairs = n_blocks * n_queries * candidates.shape[0]
    flops = 2 * pairs * terms * dim * tokens * 16
    return pl.pallas_call(
        functools.partial(score_kernel, shifts, n_blocks),
        out_shape=jax.ShapeDtypeStruct((n_blocks, n_queries, own.shape[1]), jnp.float32),
        in_specs=[SMEM] * 2 + [VMEM] * (n_blocks + 2),
        out_specs=VMEM,
        compiler_params=pltpu.CompilerParams(vmem_limit_bytes=16 << 20),
        cost_estimate=pl.CostEstimate(flops=flops, bytes_accessed=0, transcendentals=0),
        name="score",
    )(candidates, lengths, own, *blocks, documents)


def shards(queries, documents, doc_lengths, candidates):
    shard, sub = lax.axis_size("shard"), lax.axis_size("sub")
    devices = shard * sub

    def swap(value, k):
        return lax.ppermute(value, AXES, [(i, i ^ k) for i in range(devices)])

    def after(value, *others):
        return lax.optimization_barrier((value, *others))[0]

    columns = candidates.T
    own = lanes_of(candidates.shape[1], devices * candidates.shape[1])
    queries = after(queries, own)
    steps = [z * 4 for z in reversed(range(1, shard // 2))]

    def scores(shifts, blocks):
        return score(shifts, columns, doc_lengths, own, blocks, documents)

    along = {z: swap(queries, z) for z in steps}
    beside = swap(queries, 2)
    near = scores((0, 1), [queries, swap(queries, 1)])
    far = []
    tied = {z: after(along[z], near) for z in steps}
    across = {z: swap(tied[z], 2) for z in steps}
    others = {z: swap(tied[z], 1) for z in steps}
    back = []
    for z in steps:
        blocks = [along[z], others[z], across[z], swap(across[z], 1)]
        back.append(swap(scores((z, z ^ 1, z ^ 2, z ^ 3), blocks), z))
    far = scores((2, 3), [beside, swap(beside, 1)])
    near = sum((b[:2] for b in back), near)
    far = sum((b[2:] for b in back), far)
    return near[0] + swap(near[1], 1) + swap(far[0], 2) + swap(far[1], 3)


def solution(mesh):
    in_specs = (
        P(("groups", "shard", "sub"), None, None),
        P(("shard", "sub"), None, None),
        P(("shard", "sub")),
        P("groups", ("shard", "sub")),
    )
    out_specs = P(("groups", "shard", "sub"), None)
    return jax.shard_map(shards, mesh=mesh, in_specs=in_specs, out_specs=out_specs, check_vma=False)
```

```python
import functools

import jax
import jax.numpy as jnp
from jax import lax
from jax.experimental import pallas as pl
from jax.experimental.pallas import tpu as pltpu
from jax.sharding import PartitionSpec as P

AXES = ("shard", "sub")
VMEM = pl.BlockSpec(memory_space=pltpu.VMEM)
SMEM = pl.BlockSpec(memory_space=pltpu.SMEM)


def lanes_kernel(own):
    me = lax.axis_index("shard") * lax.axis_size("sub") + lax.axis_index("sub")
    lane = lax.broadcasted_iota(jnp.int32, own.shape, 1)
    slot = lax.broadcasted_iota(jnp.int32, own.shape, 0)
    own[...] = jnp.where(lane == me * own.shape[0] + slot, 1.0, 0.0)


def lanes_of(slots, width):
    return pl.pallas_call(
        lanes_kernel,
        out_shape=jax.ShapeDtypeStruct((slots, width), jnp.float32),
        out_specs=VMEM,
        compiler_params=pltpu.CompilerParams(vmem_limit_bytes=1 << 20),
        cost_estimate=pl.CostEstimate(flops=1 << 35, bytes_accessed=0, transcendentals=0),
        name="lanes",
    )()


def table_kernel(candidates, lengths, table):
    count = lengths.shape[0]
    slots, lanes = table.shape[0], 128
    for i in range(0, table.shape[1], lanes):
        named = candidates[:, i : i + lanes]
        row = jnp.maximum(named, 0)
        length = jnp.zeros_like(row)
        for j in range(0, count, lanes):
            part = jnp.broadcast_to(lengths[j : j + lanes].reshape(1, lanes), (slots, lanes))
            found = jnp.take_along_axis(part, row % lanes, axis=1)
            length = jnp.where(row // lanes == j // lanes, found, length)
        table[:, i : i + lanes] = row + jnp.where(named >= 0, length, 0) * (1 << count.bit_length())


def table_of(candidates, lengths):
    return pl.pallas_call(
        table_kernel,
        out_shape=jax.ShapeDtypeStruct(candidates.shape, candidates.dtype),
        in_specs=[VMEM] * 2,
        out_specs=VMEM,
        compiler_params=pltpu.CompilerParams(vmem_limit_bytes=1 << 20),
        name="table",
    )(candidates, lengths)


def score_kernel(shifts, n_blocks, n_known, table, own, *refs):
    blocks, documents, outs = refs[:n_blocks], refs[n_blocks], refs[n_blocks + 1 :]
    if n_known:
        known, outs = outs[0], outs[1:]
    me = lax.axis_index("shard") * lax.axis_size("sub") + lax.axis_index("sub")
    slots = table.shape[0]
    bits = documents.shape[0].bit_length()
    n_queries, terms, dim = blocks[0].shape
    tokens = documents.shape[1]
    group = dim // terms
    row = lax.broadcasted_iota(jnp.int32, (tokens, group * terms), 0)
    which = lax.broadcasted_iota(jnp.int32, (1, group * terms), 1) // terms
    member = lax.broadcasted_iota(jnp.int32, (group * terms, dim), 0) // terms
    mark = own[...]
    per = n_blocks // len(outs)
    fill = n_known // len(outs)
    for i, out in enumerate(outs):
        if n_known:
            out[:fill] = known[i * fill : (i + 1) * fill]

    def group_scores(b, first):
        column = (me ^ shifts[b]) * n_queries + first
        terms_of = blocks[b][first : first + group].reshape(group * terms, dim)
        spread = jnp.concatenate(
            [jnp.where(member == g, terms_of, jnp.zeros_like(terms_of)) for g in range(group)], 1
        )
        tops = []
        for s in range(slots):
            sides = []
            limit = jnp.zeros((1, group * terms), jnp.int32)
            for g in range(group):
                entry = table[s, column + g]
                sides.append(documents[entry & ((1 << bits) - 1)])
                limit = jnp.where(which == g, entry >> bits, limit)
            similar = lax.dot_general(
                jnp.concatenate(sides, 1),
                spread,
                (((1,), (1,)), ((), ())),
                preferred_element_type=jnp.float32,
            )
            tops.append(jnp.max(jnp.where(row < limit, similar, -jnp.inf), axis=0, keepdims=True))
        top = jnp.concatenate(tops, 0)
        top = jnp.where(top == -jnp.inf, 0.0, top)
        for g in range(group):
            total = jnp.sum(jnp.where(which == g, top, 0.0), axis=1, keepdims=True)
            line = jnp.sum(mark * total, axis=0, keepdims=True)
            outs[b // per][fill + b % per, first + g : first + g + 1, :] = line

    for b in range(n_blocks):
        for first in range(0, n_queries, group):
            group_scores(b, first)


def score(shifts, table, own, blocks, documents, known=None, n_outs=1):
    n_blocks = len(blocks)
    n_known = 0 if known is None else known.shape[0]
    n_queries, terms, dim = blocks[0].shape
    tokens = documents.shape[1]
    pairs = n_blocks * n_queries * table.shape[0]
    flops = 2 * pairs * terms * dim * tokens * 16
    tile = ((n_blocks + n_known) // n_outs, n_queries, own.shape[1])
    found = pl.pallas_call(
        functools.partial(score_kernel, shifts, n_blocks, n_known),
        out_shape=[jax.ShapeDtypeStruct(tile, jnp.float32)] * n_outs,
        in_specs=[SMEM] + [VMEM] * (n_blocks + 2 + (n_known > 0)),
        out_specs=[VMEM] * n_outs,
        compiler_params=pltpu.CompilerParams(vmem_limit_bytes=16 << 20),
        cost_estimate=pl.CostEstimate(flops=flops, bytes_accessed=0, transcendentals=0),
        name="score",
    )(table, own, *blocks, documents, *([known] if n_known else []))
    return found if n_outs > 1 else found[0]


def shards(queries, documents, doc_lengths, candidates):
    shard, sub = lax.axis_size("shard"), lax.axis_size("sub")
    devices = shard * sub

    def swap(value, k):
        return lax.ppermute(value, AXES, [(i, i ^ k) for i in range(devices)])

    def after(value, *others):
        return lax.optimization_barrier((value, *others))[0]

    table = table_of(candidates.T, doc_lengths)
    own = lanes_of(candidates.shape[1], devices * candidates.shape[1])
    queries = after(queries, own)
    steps = [z * 4 for z in reversed(range(1, shard // 2))]

    def scores(shifts, blocks, **more):
        return score(shifts, table, own, blocks, documents, **more)

    along = {z: swap(queries, z) for z in steps}
    near = scores((0, 1), [queries, swap(queries, 1)])
    beside = swap(after(queries, near), 2)
    beyond = {}
    parts = [steps[i : i + 3] for i in range(0, len(steps), 3)]
    for i, z in enumerate(steps):
        beyond[z] = swap(after(along[z], near), 2)
    back = []
    for part in parts:
        blocks, shifts = [], []
        for z in part:
            mine = after(along[z], near)
            blocks += [mine, swap(mine, 1)]
            shifts += [z, z ^ 1]
        tiles = scores(tuple(shifts), blocks)
        blocks, shifts = [], []
        for z in part:
            mine = after(beyond[z], tiles)
            blocks += [mine, swap(mine, 1)]
            shifts += [z ^ 2, z ^ 3]
        found = scores(tuple(shifts), blocks, known=tiles, n_outs=len(part))
        found = found if len(part) > 1 else [found]
        back += [swap(f, z) for f, z in zip(found, part)]
    beside = after(beside, found[0])
    far = scores((2, 3), [beside, swap(beside, 1)])
    near = sum((b[:2] for b in back), near)
    far = sum((b[2:] for b in back), far)
    return near[0] + swap(near[1], 1) + swap(far[0], 2) + swap(far[1], 3)


def solution(mesh):
    in_specs = (
        P(("groups", "shard", "sub"), None, None),
        P(("shard", "sub"), None, None),
        P(("shard", "sub")),
        P("groups", ("shard", "sub")),
    )
    out_specs = P(("groups", "shard", "sub"), None)
    return jax.shard_map(shards, mesh=mesh, in_specs=in_specs, out_specs=out_specs, check_vma=False)
```
